768 devices in a mesh: ctx: 12 (over z), tp: 8 (over x, core), grp: 8 (over y).
Axes of the slice: x: 4, y: 8, z: 12, core: 2. Of those that a mesh axis runs over, the one named last changes fastest.
Arguments:
- queries: bfloat16 [24576, 8192], P(('ctx', 'grp'), 'tp'), may hold values from -24 to 24
- keys: bfloat16 [24576, 1024], P(('ctx', 'grp'), 'tp'), may hold values from -4 to 4
- values: bfloat16 [24576, 1024], P(('ctx', 'grp'), 'tp'), may hold values from -6 to 6
- output_gradient: bfloat16 [24576, 8192], P(('ctx', 'grp'), 'tp'), may hold values from -6 to 6
- doc_tiles: int32 [32], replicated, may hold values from 1 to 8, 192 in all
- doc_pads: int32 [32], replicated, may hold values from 0 to 127
Outputs:
- grad_queries: bfloat16 [24576, 8192], P(('ctx', 'grp'), 'tp')
- grad_keys: bfloat16 [24576, 1024], P(('ctx', 'grp'), 'tp')
- grad_values: bfloat16 [24576, 1024], P(('ctx', 'grp'), 'tp')
The draws below stay inside these ranges and needn't reach their ends.
All inputs are finite; a program needn't handle non-finite values.
Results may differ from the reference program's by a relative error of at most 0.0081.
Values may be sent and summed in bfloat16 or wider, within the bound.
A program may use at most 64 MiB of HBM per device.

```python
import math
import jax
import jax.numpy as jnp
import numpy as np
from jax import lax

QUERY_HEADS = 64
KEY_VALUE_HEADS = 8
HEAD_SIZE = 128
TILE = 128
TILES_DEV = 2
CAP = 8
REACH = 4
TILES = 192
SEQUENCE_TOKENS = 24576
NDOC = 32


def draw_queries(key, part):
    key = jax.random.fold_in(key, 1)
    drawn_block = jnp.clip(jax.random.normal(key, (SEQUENCE_TOKENS, QUERY_HEADS * HEAD_SIZE), jnp.float32), -5.0, 5.0)
    return drawn_block.astype(jnp.bfloat16)


def draw_keys(key, part):
    key = jax.random.fold_in(key, 2)
    drawn_block = jnp.clip(jax.random.normal(key, (SEQUENCE_TOKENS, KEY_VALUE_HEADS * HEAD_SIZE), jnp.float32), -4.0, 4.0)
    return drawn_block.astype(jnp.bfloat16)


def set_ends(values, own_key, least, top_value):
    index_at = [jax.random.randint(jax.random.fold_in(own_key, axis), (), 0, length) for axis, length in enumerate(values.shape)]
    main_axis = values.shape.index(max(values.shape))
    next_to = index_at[:main_axis] + [(index_at[main_axis] + 1) % values.shape[main_axis]] + index_at[main_axis + 1:]
    return values.at[tuple(index_at)].set(least).at[tuple(next_to)].set(top_value)


def block_levels(stream_key, shape, split, low, top_value):
    factor_of = 1.0
    for position, parts in split:
        heights = jax.random.uniform(jax.random.fold_in(jax.random.fold_in(stream_key, 6), position), (parts,), jnp.float32, low / len(split), top_value / len(split))
        factor_of = factor_of * jnp.repeat(jnp.exp(heights), shape[position] // parts).reshape((-1,) + (1,) * (len(shape) - 1 - position))
    return factor_of


def length_profile(amount, total, most, slope):
    weights = [(1 << 20) // math.isqrt(rank ** slope) + 1 for rank in range(2, amount + 1)]
    spare, counts = total - most - (amount - 1), [1] * (amount - 1)
    while spare > 0:
        movable = [i for i in range(amount - 1) if counts[i] < most]
        pool, left = sum([weights[i] for i in movable]), spare
        for i in movable:
            extra = min(most - counts[i], max(1, left * weights[i] // pool), spare)
            counts[i] = counts[i] + extra
            spare = spare - extra
    return np.array([most] + counts)


def uneven(stream_key, count, total, limit, skew):
    if count == 2:
        one = jax.random.randint(stream_key, (), max(1, total - limit), min(limit, total - 1) + 1)
        return jnp.stack([one, total - one])
    sizes = jnp.asarray(length_profile(count, total, limit, skew), jnp.int32)
    twos = (count - 1) // 2
    giver, taker = sizes[1:1 + 2 * twos:2], sizes[2:2 + 2 * twos:2]
    room = jnp.minimum(giver - 1, limit - taker)
    moved = jax.random.randint(jax.random.fold_in(stream_key, 1), (twos,), 0, 1 << 20) % (room + 1)
    sizes = sizes.at[1:1 + 2 * twos:2].set(giver - moved).at[2:2 + 2 * twos:2].set(taker + moved)
    return sizes[jax.random.permutation(jax.random.fold_in(stream_key, 2), count)]


def noise(rng, shape, width, reach, cuts=(), held_as=jnp.bfloat16):
    gain = block_levels(rng, shape, cuts, -0.22, 0.18) if cuts else 1.0
    result = jax.random.normal(rng, shape, jnp.float32) * width * gain
    return jnp.minimum(jnp.maximum(result, -reach), reach).astype(held_as)


def setup_inputs(seed: int = 0) -> dict:
    key_of = jax.random.split(jax.random.key(seed), 7)
    return {
        "queries": draw_queries(jax.random.fold_in(key_of[6], 71), 0),
        "keys": draw_keys(jax.random.fold_in(key_of[6], 71), 0),
        "values": noise(key_of[2], (SEQUENCE_TOKENS, KEY_VALUE_HEADS * HEAD_SIZE), 1.0, 6.0, ((0, 96), (1, 8))),
        "output_gradient": noise(key_of[3], (SEQUENCE_TOKENS, QUERY_HEADS * HEAD_SIZE), 1.0, 6.0, ((0, 96), (1, 8))),
        "doc_tiles": uneven(key_of[4], NDOC, TILES, CAP, 2).astype(jnp.int32),
        "doc_pads": set_ends(jax.random.randint(key_of[5], (NDOC,), 0, TILE), jax.random.fold_in(key_of[5], 1), 0, TILE - 1).astype(jnp.int32),
    }


def token_table(doc_tiles, doc_pads, index):
    count = doc_tiles.shape[0]
    starts = (jnp.cumsum(doc_tiles, dtype=jnp.int32) - doc_tiles) * TILE
    ends = starts + doc_tiles * TILE - doc_pads
    found = (starts[None, :] <= index[:, None]).astype(jnp.int32)
    doc = lax.optimization_barrier(jnp.sum(found, axis=1, dtype=jnp.int32)) - 1
    match = (doc[:, None] == jnp.arange(count, dtype=jnp.int32)[None, :]).astype(jnp.int32)
    end_of = lax.optimization_barrier(jnp.sum(match * ends[None, :], axis=1, dtype=jnp.int32))
    live = (doc >= 0) & (index < end_of)
    return (doc, live)

def attend(qh, kh, vh, gh, qidx, kidx, qdoc, qok, kdoc, kok):
    scale = 1.0 / jnp.sqrt(jnp.float32(qh.shape[-1]))
    allowed = (qdoc[:, None] == kdoc[None, :]) & qok[:, None] & kok[None, :] & (kidx[None, :] <= qidx[:, None])
    qf = qh.astype(jnp.float32)
    kf = kh.astype(jnp.float32)
    vf = vh.astype(jnp.float32)
    gf = gh.astype(jnp.float32)
    scores = jnp.einsum('qgd,kd->gqk', qf, kf) * scale
    masked = jnp.where(allowed[None], scores, jnp.float32(-1e+30))
    top = lax.optimization_barrier(jnp.max(masked, axis=-1, keepdims=True))
    weights = jnp.where(allowed[None], jnp.exp(masked - top), jnp.float32(0.0))
    total = lax.optimization_barrier(jnp.sum(weights, axis=-1))
    total = jnp.where(qok[None, :], total, jnp.float32(1.0))
    probs = (weights / total[..., None]).astype(jnp.bfloat16)
    pf = probs.astype(jnp.float32)
    out = jnp.einsum('gqk,kd->qgd', pf, vf)
    delta = lax.optimization_barrier(jnp.sum(gf * out, axis=-1))
    dprob = jnp.einsum('qgd,kd->gqk', gf, vf)
    dscore = (pf * (dprob - jnp.transpose(delta)[..., None])).astype(jnp.bfloat16)
    sf = dscore.astype(jnp.float32)
    grad_q = jnp.einsum('gqk,kd->qgd', sf, kf) * scale
    key_gradient = jnp.einsum('gqk,qgd->kd', sf, qf) * scale
    value_gradient = jnp.einsum('gqk,qgd->kd', pf, gf)
    return (grad_q, key_gradient, value_gradient)

def reference(queries, keys, values, output_gradient, doc_tiles, doc_pads):
    block_span = TILES_DEV * TILE
    count = SEQUENCE_TOKENS // block_span
    leading_part = REACH * block_span
    window_width = (REACH + 1) * block_span
    head_group = QUERY_HEADS // KEY_VALUE_HEADS
    index = jnp.arange(SEQUENCE_TOKENS, dtype=jnp.int32)
    qdoc_all, qok_all = token_table(doc_tiles, doc_pads, index)
    kidx_all = jnp.arange(-leading_part, SEQUENCE_TOKENS, dtype=jnp.int32)
    kdoc_all, kok_all = token_table(doc_tiles, doc_pads, kidx_all)
    zero_key_value = jnp.zeros((leading_part, KEY_VALUE_HEADS * HEAD_SIZE), jnp.bfloat16)
    padded_keys = jnp.concatenate([zero_key_value, keys], axis=0)
    padded_values = jnp.concatenate([zero_key_value, values], axis=0)

    def step(carry, number):
        dk_acc, dv_acc = carry
        start_index = (number * block_span).astype(jnp.int32)
        query_block = lax.dynamic_slice_in_dim(queries, start_index, block_span, 0).reshape(block_span, KEY_VALUE_HEADS, head_group, HEAD_SIZE)
        gradient_block = lax.dynamic_slice_in_dim(output_gradient, start_index, block_span, 0).reshape(block_span, KEY_VALUE_HEADS, head_group, HEAD_SIZE)
        key_window = lax.dynamic_slice_in_dim(padded_keys, start_index, window_width, 0).reshape(window_width, KEY_VALUE_HEADS, HEAD_SIZE)
        value_window = lax.dynamic_slice_in_dim(padded_values, start_index, window_width, 0).reshape(window_width, KEY_VALUE_HEADS, HEAD_SIZE)
        qidx = lax.dynamic_slice_in_dim(index, start_index, block_span, 0)
        qdoc = lax.dynamic_slice_in_dim(qdoc_all, start_index, block_span, 0)
        qok = lax.dynamic_slice_in_dim(qok_all, start_index, block_span, 0)
        kidx = lax.dynamic_slice_in_dim(kidx_all, start_index, window_width, 0)
        kdoc = lax.dynamic_slice_in_dim(kdoc_all, start_index, window_width, 0)
        kok = lax.dynamic_slice_in_dim(kok_all, start_index, window_width, 0)

        def head(pieces):
            qh, kh, vh, gh = pieces
            return attend(qh, kh, vh, gh, qidx, kidx, qdoc, qok, kdoc, kok)
        grad_q, key_gradient, value_gradient = lax.map(head, (jnp.transpose(query_block, (1, 0, 2, 3)), jnp.transpose(key_window, (1, 0, 2)), jnp.transpose(value_window, (1, 0, 2)), jnp.transpose(gradient_block, (1, 0, 2, 3))))
        grad_q = jnp.transpose(grad_q, (1, 0, 2, 3)).reshape(block_span, QUERY_HEADS * HEAD_SIZE).astype(jnp.bfloat16)
        key_gradient = jnp.transpose(key_gradient, (1, 0, 2)).reshape(window_width, KEY_VALUE_HEADS * HEAD_SIZE)
        value_gradient = jnp.transpose(value_gradient, (1, 0, 2)).reshape(window_width, KEY_VALUE_HEADS * HEAD_SIZE)
        dk_acc = lax.dynamic_update_slice_in_dim(dk_acc, lax.dynamic_slice_in_dim(dk_acc, start_index, window_width, 0) + key_gradient, start_index, 0)
        dv_acc = lax.dynamic_update_slice_in_dim(dv_acc, lax.dynamic_slice_in_dim(dv_acc, start_index, window_width, 0) + value_gradient, start_index, 0)
        return ((dk_acc, dv_acc), grad_q)
    vacant_block = jnp.zeros((SEQUENCE_TOKENS + leading_part, KEY_VALUE_HEADS * HEAD_SIZE), jnp.float32)
    (dk_acc, dv_acc), grad_blocks = lax.scan(step, (vacant_block, vacant_block), jnp.arange(count, dtype=jnp.int32))
    grad_queries = grad_blocks.reshape(SEQUENCE_TOKENS, QUERY_HEADS * HEAD_SIZE)
    return (grad_queries, dk_acc[leading_part:].astype(jnp.bfloat16), dv_acc[leading_part:].astype(jnp.bfloat16))
```

```python
import functools
import math

import jax
import jax.numpy as jnp
from jax import lax
from jax.experimental import pallas as pl
from jax.experimental.pallas import tpu as pltpu
from jax.sharding import PartitionSpec as P

HEAD = 128
TILE = 128
SLOTS = 9
AHEAD = 7
NEG = -1e30
F32 = jnp.float32
BF16 = jnp.bfloat16


VALUE_STEPS = (
    ("part", 0), ("back", 0), ("part", 1), ("back", 1), ("move", 5), ("part", 2), ("back", 2),
    ("move", 6), ("part", 7), ("part", 3), ("back", 3), ("move", 3), ("dprob", 7), ("part", 8),
    ("part", 4), ("back", 4), ("move", 4), ("dprob", 8), ("part", 5), ("back", 5), ("move", 1),
    ("dprob", 5), ("part", 6), ("back", 6), ("move", 2), ("dprob", 6), ("dprob", 3), ("dprob", 4),
    ("back", 7), ("back", 8), ("dprob", 1), ("dprob", 2), ("move", 0), ("dprob", 0),
)
KEY_STEPS = (
    ("part", 0), ("back", 0), ("part", 1), ("back", 1), ("part", 2), ("back", 2), ("part", 3),
    ("part", 4), ("back", 3), ("part", 5), ("part", 6), ("back", 4), ("part", 7), ("part", 8),
    ("back", 5), ("query", 0), ("back", 6), ("query", 1), ("back", 7), ("back", 8),
)


def kernel(
    tiles_hbm, pads_hbm, q_hbm, k_hbm, v_hbm, g_hbm,
    dq_out, dk_out, dv_out,
    tiles_ref, pads_ref, q, g, qt, gt, kw, vw, kt, e, p, m_ref, l_ref, f_ref, d_ref, sv, rv, sk, rk,
    local_sem, kss, krs, vss, vrs, svs, rvs, sks, rks,
):
    ctx, grp = lax.axis_index("ctx"), lax.axis_index("grp")
    nctx, ngrp = lax.axis_size("ctx"), lax.axis_size("grp")
    heads = q_hbm.shape[1] // HEAD
    cols = heads * TILE
    pairs = heads // 2
    scale = 1.0 / math.sqrt(HEAD)
    c2 = scale * math.log2(math.e)
    mine = ctx * ngrp + grp
    up_grp = lax.rem(grp + 1, ngrp)
    up_ctx = lax.rem(ctx + jnp.where(grp == ngrp - 1, 1, 0), nctx)
    dn_grp = lax.rem(grp + ngrp - 1, ngrp)
    dn_ctx = lax.rem(ctx + jnp.where(grp == 0, nctx - 1, 0), nctx)
    nxt = {"ctx": up_ctx, "grp": up_grp}
    prv = {"ctx": dn_ctx, "grp": dn_grp}

    own = pl.ds(AHEAD * TILE, 2 * TILE)
    loads = [
        pltpu.make_async_copy(src, dst, local_sem.at[n])
        for n, (src, dst) in enumerate(
            (
                (k_hbm, kw.at[own]), (q_hbm, q), (v_hbm, vw.at[own]), (g_hbm, g),
                (tiles_hbm, tiles_ref), (pads_hbm, pads_ref),
            )
        )
    ]
    for load in loads:
        load.start()

    barrier = pltpu.get_barrier_semaphore()
    for other in (nxt, prv):
        pl.semaphore_signal(barrier, inc=1, device_id=other, device_id_type=pl.DeviceIdType.MESH)
    pl.semaphore_wait(barrier, 2)

    def ahead(win, ssem, rsem, dst):
        return pltpu.make_async_remote_copy(
            src_ref=win.at[pl.ds((dst + 2) * TILE, TILE)],
            dst_ref=win.at[pl.ds(dst * TILE, TILE)],
            send_sem=ssem.at[dst],
            recv_sem=rsem.at[dst],
            device_id=nxt,
            device_id_type=pl.DeviceIdType.MESH,
        )

    def back(sbuf, rbuf, ssem, rsem, slot):
        return pltpu.make_async_remote_copy(
            src_ref=sbuf.at[slot],
            dst_ref=rbuf.at[slot],
            send_sem=ssem.at[slot],
            recv_sem=rsem.at[slot],
            device_id=prv,
            device_id_type=pl.DeviceIdType.MESH,
        )

    k_move = [ahead(kw, kss, krs, dst) for dst in range(AHEAD)]
    v_move = [ahead(vw, vss, vrs, dst) for dst in range(AHEAD)]
    v_back = [back(sv, rv, svs, rvs, slot) for slot in range(AHEAD)]
    k_back = [back(sk, rk, sks, rks, slot) for slot in range(AHEAD)]

    loads[0].wait()
    k_move[5].start()
    k_move[6].start()

    loads[4].wait()
    loads[5].wait()
    first = [jnp.int32(0), jnp.int32(0)]
    stop = [jnp.int32(0), jnp.int32(0)]
    at = jnp.int32(0)
    for j in range(tiles_ref.shape[0]):
        after = at + tiles_ref[j]
        end = after * TILE - pads_ref[j]
        for i in range(2):
            tile = 2 * mine + i
            inside = (at <= tile) & (tile < after)
            first[i] = jnp.where(inside, at, first[i])
            stop[i] = jnp.where(inside, end, stop[i])
        at = after

    def rows_of(slot):
        return pl.ds(slot * TILE, TILE)

    def cols_of(i, c):
        return pl.ds(pl.multiple_of(i * cols + c * 2 * TILE, TILE), 2 * TILE)

    def two_heads(ref, i, c):
        at_row = pl.ds(i * TILE, TILE)
        return jnp.concatenate(
            [
                ref[at_row, pl.ds(pl.multiple_of((2 * c + n) * HEAD, HEAD), HEAD)]
                for n in range(2)
            ],
            axis=0,
        )

    def tiles_of(slot):
        return [i for i in range(2) if i <= slot <= AHEAD + i]

    def over_pairs(body, init=0):
        return lax.fori_loop(0, pairs, body, init, unroll=True)

    def scores(slot):
        def step(c, carry):
            key = kw[rows_of(slot)]
            for i in tiles_of(slot):
                s = jnp.dot(key, qt[:, cols_of(i, c)], preferred_element_type=F32)
                if slot == AHEAD + i:
                    row = lax.broadcasted_iota(jnp.int32, s.shape, 0)
                    col = lax.broadcasted_iota(jnp.int32, s.shape, 1)
                    s = jnp.where(row <= (col & (TILE - 1)), s, NEG)
                top = jnp.max(s, axis=0, keepdims=True) * c2
                w = jnp.exp2(s * c2 - top)
                e[rows_of(slot), cols_of(i, c)] = w
                m_ref[pl.ds(slot, 1), cols_of(i, c)] = top
                l_ref[pl.ds(slot, 1), cols_of(i, c)] = jnp.sum(w, axis=0, keepdims=True)
            return carry

        over_pairs(step)
        kt[:, rows_of(slot)] = jnp.transpose(kw[rows_of(slot)])

    def factors():
        for i in range(2):
            part = pl.ds(i * cols, cols)
            shape = (16, cols)
            row = lax.broadcasted_iota(jnp.int32, shape, 0)
            token = lax.broadcasted_iota(jnp.int32, shape, 1) & (TILE - 1)
            tile = 2 * mine + i
            valid = (row >= i) & (row <= AHEAD + i) & (row + (2 * mine - AHEAD) >= first[i])
            tops = jnp.where(valid, m_ref[:, part], NEG)
            w = jnp.exp2(tops - jnp.max(tops, axis=0, keepdims=True))
            total = jnp.sum(w * jnp.where(valid, l_ref[:, part], 0.0), axis=0, keepdims=True)
            live = token < stop[i] - tile * TILE
            f_ref[:, part] = jnp.where(live, w / total, 0.0)

    def value_part(slot):
        def step(c, acc):
            for i in tiles_of(slot):
                w = e[rows_of(slot), cols_of(i, c)] * f_ref[pl.ds(slot, 1), cols_of(i, c)]
                w = w.astype(BF16)
                p[rows_of(slot), cols_of(i, c)] = w
                acc = acc + jnp.dot(w, two_heads(g, i, c), preferred_element_type=F32)
            return acc

        return over_pairs(step, jnp.zeros((TILE, HEAD), F32))

    def dprobs(slot):
        def step(c, carry):
            value = vw[rows_of(slot)]
            for i in tiles_of(slot):
                d = jnp.dot(value, gt[:, cols_of(i, c)], preferred_element_type=F32)
                e[rows_of(slot), cols_of(i, c)] = d
                d = d * p[rows_of(slot), cols_of(i, c)].astype(F32)
                d_ref[pl.ds(slot, 1), cols_of(i, c)] = jnp.sum(d, axis=0, keepdims=True)
            return carry

        over_pairs(step)

    def deltas():
        for i in range(2):
            part = pl.ds(i * cols, cols)
            row = lax.broadcasted_iota(jnp.int32, (16, cols), 0)
            terms = jnp.where((row >= i) & (row <= AHEAD + i), d_ref[:, part], 0.0)
            f_ref[:, part] = jnp.broadcast_to(jnp.sum(terms, axis=0, keepdims=True), (16, cols))

    def key_part(slot):
        def step(c, acc):
            for i in tiles_of(slot):
                d = e[rows_of(slot), cols_of(i, c)] - f_ref[pl.ds(0, 1), cols_of(i, c)]
                d = (p[rows_of(slot), cols_of(i, c)].astype(F32) * d).astype(BF16)
                p[rows_of(slot), cols_of(i, c)] = d
                acc = acc + jnp.dot(d, two_heads(q, i, c), preferred_element_type=F32)
            return acc

        return over_pairs(step, jnp.zeros((TILE, HEAD), F32)) * scale

    def query_part(i, dq):
        window = pl.ds(i * TILE, (SLOTS - 1) * TILE)

        def step(c, carry):
            t = jnp.dot(kt[:, window], p[window, cols_of(i, c)], preferred_element_type=F32) * scale
            for n in range(2):
                head = pl.ds(pl.multiple_of((2 * c + n) * HEAD, HEAD), HEAD)
                t_head = t[:, n * TILE : (n + 1) * TILE]
                dq[pl.ds(i * TILE, TILE), head] = jnp.transpose(t_head).astype(BF16)
            return carry

        over_pairs(step)

    def returned(part, slot, moves, sbuf, rbuf, out):
        if slot >= 2:
            moves[slot - 2].wait_recv()
            part = part + rbuf[slot - 2].astype(F32)
        if slot < AHEAD:
            sbuf[slot] = part.astype(BF16)
            moves[slot].start()
        else:
            out[pl.ds((slot - AHEAD) * TILE, TILE), :] = part.astype(BF16)

    def passed_on(moves, slot):
        moves[slot].wait_recv()
        if slot >= 2:
            moves[slot - 2].start()

    def turned(ref, out):
        def step(c, carry):
            for i in range(2):
                for n in range(2):
                    head = pl.ds(pl.multiple_of((2 * c + n) * HEAD, HEAD), HEAD)
                    at_col = pl.ds(pl.multiple_of(i * cols + (2 * c + n) * TILE, TILE), TILE)
                    out[:, at_col] = jnp.transpose(ref[pl.ds(i * TILE, TILE), head])
            return carry

        over_pairs(step)

    loads[1].wait()
    turned(q, qt)
    loads[3].wait()
    turned(g, gt)
    for slot, done in ((5, 7), (6, 8), (3, 5), (4, 6), (1, 3), (2, 4)):
        passed_on(k_move, slot)
        if slot == 2:
            loads[2].wait()
            v_move[5].start()
            v_move[6].start()
        scores(done)
    scores(1)
    scores(2)
    passed_on(k_move, 0)
    scores(0)
    factors()

    parts = {}
    for what, slot in VALUE_STEPS:
        if what == "part":
            parts[slot] = value_part(slot)
        elif what == "back":
            returned(parts.pop(slot), slot, v_back, sv, rv, dv_out)
        elif what == "move":
            passed_on(v_move, slot)
        else:
            dprobs(slot)
    deltas()

    for what, slot in KEY_STEPS:
        if what == "part":
            parts[slot] = key_part(slot)
        elif what == "back":
            returned(parts.pop(slot), slot, k_back, sk, rk, dk_out)
        else:
            query_part(slot, dq_out)

    for moves in (k_move, v_move, v_back, k_back):
        for move in moves:
            move.wait_send()


def shards(queries, keys, values, output_gradient, doc_tiles, doc_pads):
    rows, wide = queries.shape
    window = SLOTS * TILE
    both = 2 * (wide // HEAD) * TILE
    anywhere = pl.BlockSpec(memory_space=pl.ANY)
    vmem = pl.BlockSpec(memory_space=pltpu.VMEM)
    dma = pltpu.SemaphoreType.DMA
    operands = (doc_tiles, doc_pads, queries, keys, values, output_gradient)
    return pl.pallas_call(
        kernel,
        out_shape=(
            jax.ShapeDtypeStruct((rows, wide), BF16),
            jax.ShapeDtypeStruct(keys.shape, BF16),
            jax.ShapeDtypeStruct(values.shape, BF16),
        ),
        in_specs=[anywhere] * 6,
        out_specs=(vmem, vmem, vmem),
        scratch_shapes=[
            pltpu.SMEM(doc_tiles.shape, jnp.int32),
            pltpu.SMEM(doc_pads.shape, jnp.int32),
            pltpu.VMEM((rows, wide), BF16),
            pltpu.VMEM((rows, wide), BF16),
            pltpu.VMEM((HEAD, both), BF16),
            pltpu.VMEM((HEAD, both), BF16),
            pltpu.VMEM((window, HEAD), BF16),
            pltpu.VMEM((window, HEAD), BF16),
            pltpu.VMEM((HEAD, window), BF16),
            pltpu.VMEM((window, both), F32),
            pltpu.VMEM((window, both), BF16),
            pltpu.VMEM((16, both), F32),
            pltpu.VMEM((16, both), F32),
            pltpu.VMEM((16, both), F32),
            pltpu.VMEM((16, both), F32),
        ]
        + [pltpu.VMEM((AHEAD, TILE, HEAD), BF16)] * 4
        + [dma((6,))]
        + [dma((AHEAD,))] * 8,
        compiler_params=pltpu.CompilerParams(
            collective_id=0, has_side_effects=True, vmem_limit_bytes=48 * 1024 * 1024
        ),
        cost_estimate=pl.CostEstimate(flops=2_700_000_000, bytes_accessed=2_400_000, transcendentals=2_100_000),
        name="attention_backward",
    )(*[pltpu.with_memory_space_constraint(x, pltpu.HBM) for x in operands])


def solution(mesh):
    split = P(("ctx", "grp"), "tp")
    return jax.shard_map(
        shards,
        mesh=mesh,
        in_specs=(split, split, split, split, P(), P()),
        out_specs=(split, split, split),
        check_vma=False,
    )
```

```python
import functools
import math

import jax
import jax.numpy as jnp
from jax import lax
from jax.experimental import pallas as pl
from jax.experimental.pallas import tpu as pltpu
from jax.sharding import PartitionSpec as P

HEAD = 128
TILE = 128
SLOTS = 9
AHEAD = 7
NEG = -1e30
F32 = jnp.float32
BF16 = jnp.bfloat16


BACK = (4, 3, 3, 2, 2, 1, 1)
HOME = (4, 1, 1, 2, 2, 1, 1)


def kernel(
    tiles_hbm, pads_hbm, q_hbm, k_hbm, v_hbm, g_hbm,
    dq_out, dk_out, dv_out,
    tiles_ref, pads_ref, q, g, qt, gt, kw, vw, kt, e, p, m_ref, l_ref, f_ref, d_ref, sv, rv, sk, rk,
    local_sem, kss, krs, vss, vrs, svs, rvs, sks, rks,
):
    ctx, grp = lax.axis_index("ctx"), lax.axis_index("grp")
    nctx, ngrp = lax.axis_size("ctx"), lax.axis_size("grp")
    heads = q_hbm.shape[1] // HEAD
    cols = heads * TILE
    pairs = heads // 2
    scale = 1.0 / math.sqrt(HEAD)
    c2 = scale * math.log2(math.e)
    mine = ctx * ngrp + grp
    shards_all = nctx * ngrp

    def shard(distance):
        index = mine + distance
        return {"ctx": index // ngrp, "grp": index % ngrp}

    own = pl.ds(AHEAD * TILE, 2 * TILE)
    loads = [
        pltpu.make_async_copy(src, dst, local_sem.at[n])
        for n, (src, dst) in enumerate(
            (
                (k_hbm, kw.at[own]), (q_hbm, q), (v_hbm, vw.at[own]), (g_hbm, g),
                (tiles_hbm, tiles_ref), (pads_hbm, pads_ref),
            )
        )
    ]
    for load in loads:
        load.start()

    @pl.when(mine < 4)
    def _():
        kw[pl.ds(0, AHEAD * TILE)] = jnp.zeros((AHEAD * TILE, HEAD), BF16)
        vw[pl.ds(0, AHEAD * TILE)] = jnp.zeros((AHEAD * TILE, HEAD), BF16)

    @pl.when(mine >= shards_all - 4)
    def _():
        rv[...] = jnp.zeros(rv.shape, BF16)
        rk[...] = jnp.zeros(rk.shape, BF16)

    barrier = pltpu.get_barrier_semaphore()
    partners = jnp.int32(0)
    for distance in (1, 2, 4):
        for to, there in ((distance, mine + distance < shards_all), (-distance, mine >= distance)):
            @pl.when(there)
            def _():
                pl.semaphore_signal(
                    barrier, inc=1, device_id=shard(to), device_id_type=pl.DeviceIdType.MESH
                )
            partners = partners + jnp.where(there, 1, 0)
    pl.semaphore_wait(barrier, partners)

    class Move:
        def __init__(self, src, dst, ssem, rsem, to, sends, receives):
            self.copy = pltpu.make_async_remote_copy(
                src_ref=src, dst_ref=dst, send_sem=ssem, recv_sem=rsem,
                device_id=shard(to), device_id_type=pl.DeviceIdType.MESH,
            )
            self.sends, self.receives = sends, receives

        def start(self):
            pl.when(self.sends)(self.copy.start)

        def wait_send(self):
            pl.when(self.sends)(self.copy.wait_send)

        def wait_recv(self):
            pl.when(self.receives)(self.copy.wait_recv)

    def ahead(win, ssem, rsem, dst):
        back = BACK[dst]
        step = 1 if back == 3 else back
        src = dst + 2 if back == 3 else (AHEAD + 1 if dst % 2 == 0 else AHEAD)
        sends = mine + step < shards_all
        if back == 3:
            sends = sends & (mine >= 2)
        return Move(
            win.at[pl.ds(src * TILE, TILE)], win.at[pl.ds(dst * TILE, TILE)],
            ssem.at[dst], rsem.at[dst], step, sends, mine >= back,
        )

    def home(sbuf, rbuf, ssem, rsem, slot):
        receives = mine + HOME[slot] < shards_all
        if BACK[slot] == 3:
            receives = receives & (mine >= 2)
        return Move(
            sbuf.at[slot], rbuf.at[slot], ssem.at[slot], rsem.at[slot],
            -HOME[slot], mine >= BACK[slot], receives,
        )

    k_move = [ahead(kw, kss, krs, dst) for dst in range(AHEAD)]
    v_move = [ahead(vw, vss, vrs, dst) for dst in range(AHEAD)]
    v_home = [home(sv, rv, svs, rvs, slot) for slot in range(AHEAD)]
    k_home = [home(sk, rk, sks, rks, slot) for slot in range(AHEAD)]

    loads[0].wait()
    for slot in (3, 4, 5, 6, 0):
        k_move[slot].start()
    loads[2].wait()
    for slot in (3, 4):
        v_move[slot].start()

    loads[4].wait()
    loads[5].wait()
    first = [jnp.int32(0), jnp.int32(0)]
    stop = [jnp.int32(0), jnp.int32(0)]
    at = jnp.int32(0)
    for j in range(tiles_ref.shape[0]):
        after = at + tiles_ref[j]
        end = after * TILE - pads_ref[j]
        for i in range(2):
            tile = 2 * mine + i
            inside = (at <= tile) & (tile < after)
            first[i] = jnp.where(inside, at, first[i])
            stop[i] = jnp.where(inside, end, stop[i])
        at = after

    def rows_of(slot):
        return pl.ds(slot * TILE, TILE)

    def cols_of(i, c):
        return pl.ds(pl.multiple_of(i * cols + c * 2 * TILE, TILE), 2 * TILE)

    def two_heads(ref, i, c):
        at_row = pl.ds(i * TILE, TILE)
        return jnp.concatenate(
            [
                ref[at_row, pl.ds(pl.multiple_of((2 * c + n) * HEAD, HEAD), HEAD)]
                for n in range(2)
            ],
            axis=0,
        )

    def tiles_of(slot):
        return [i for i in range(2) if i <= slot <= AHEAD + i]

    def over_pairs(body, init=0):
        return lax.fori_loop(0, pairs, body, init, unroll=True)

    def scores(slot):
        def step(c, carry):
            key = kw[rows_of(slot)]
            for i in tiles_of(slot):
                s = jnp.dot(key, qt[:, cols_of(i, c)], preferred_element_type=F32)
                if slot == AHEAD + i:
                    row = lax.broadcasted_iota(jnp.int32, s.shape, 0)
                    col = lax.broadcasted_iota(jnp.int32, s.shape, 1)
                    s = jnp.where(row <= (col & (TILE - 1)), s, NEG)
                top = jnp.max(s, axis=0, keepdims=True) * c2
                w = jnp.exp2(s * c2 - top)
                e[rows_of(slot), cols_of(i, c)] = w
                m_ref[pl.ds(slot, 1), cols_of(i, c)] = top
                l_ref[pl.ds(slot, 1), cols_of(i, c)] = jnp.sum(w, axis=0, keepdims=True)
            return carry

        over_pairs(step)
        kt[:, rows_of(slot)] = jnp.transpose(kw[rows_of(slot)])

    def factors():
        for i in range(2):
            part = pl.ds(i * cols, cols)
            shape = (16, cols)
            row = lax.broadcasted_iota(jnp.int32, shape, 0)
            token = lax.broadcasted_iota(jnp.int32, shape, 1) & (TILE - 1)
            tile = 2 * mine + i
            valid = (row >= i) & (row <= AHEAD + i) & (row + (2 * mine - AHEAD) >= first[i])
            tops = jnp.where(valid, m_ref[:, part], NEG)
            w = jnp.exp2(tops - jnp.max(tops, axis=0, keepdims=True))
            total = jnp.sum(w * jnp.where(valid, l_ref[:, part], 0.0), axis=0, keepdims=True)
            live = token < stop[i] - tile * TILE
            f_ref[:, part] = jnp.where(live, w / total, 0.0)

    def value_part(slot):
        def step(c, acc):
            for i in tiles_of(slot):
                w = e[rows_of(slot), cols_of(i, c)] * f_ref[pl.ds(slot, 1), cols_of(i, c)]
                w = w.astype(BF16)
                p[rows_of(slot), cols_of(i, c)] = w
                acc = acc + jnp.dot(w, two_heads(g, i, c), preferred_element_type=F32)
            return acc

        return over_pairs(step, jnp.zeros((TILE, HEAD), F32))

    def dprobs(slot):
        def step(c, carry):
            value = vw[rows_of(slot)]
            for i in tiles_of(slot):
                d = jnp.dot(value, gt[:, cols_of(i, c)], preferred_element_type=F32)
                e[rows_of(slot), cols_of(i, c)] = d
                d = d * p[rows_of(slot), cols_of(i, c)].astype(F32)
                d_ref[pl.ds(slot, 1), cols_of(i, c)] = jnp.sum(d, axis=0, keepdims=True)
            return carry

        over_pairs(step)

    def deltas():
        for i in range(2):
            part = pl.ds(i * cols, cols)
            row = lax.broadcasted_iota(jnp.int32, (16, cols), 0)
            terms = jnp.where((row >= i) & (row <= AHEAD + i), d_ref[:, part], 0.0)
            f_ref[:, part] = jnp.broadcast_to(jnp.sum(terms, axis=0, keepdims=True), (16, cols))

    def key_part(slot):
        def step(c, acc):
            for i in tiles_of(slot):
                d = e[rows_of(slot), cols_of(i, c)] - f_ref[pl.ds(0, 1), cols_of(i, c)]
                d = (p[rows_of(slot), cols_of(i, c)].astype(F32) * d).astype(BF16)
                p[rows_of(slot), cols_of(i, c)] = d
                acc = acc + jnp.dot(d, two_heads(q, i, c), preferred_element_type=F32)
            return acc

        return over_pairs(step, jnp.zeros((TILE, HEAD), F32)) * scale

    def query_part(i, dq):
        window = pl.ds(i * TILE, (SLOTS - 1) * TILE)

        def step(c, carry):
            t = jnp.dot(kt[:, window], p[window, cols_of(i, c)], preferred_element_type=F32) * scale
            for n in range(2):
                head = pl.ds(pl.multiple_of((2 * c + n) * HEAD, HEAD), HEAD)
                t_head = t[:, n * TILE : (n + 1) * TILE]
                dq[pl.ds(i * TILE, TILE), head] = jnp.transpose(t_head).astype(BF16)
            return carry

        over_pairs(step)

    def turned(ref, out):
        def step(c, carry):
            for i in range(2):
                for n in range(2):
                    head = pl.ds(pl.multiple_of((2 * c + n) * HEAD, HEAD), HEAD)
                    at_col = pl.ds(pl.multiple_of(i * cols + (2 * c + n) * TILE, TILE), TILE)
                    out[:, at_col] = jnp.transpose(ref[pl.ds(i * TILE, TILE), head])
            return carry

        over_pairs(step)

    def arrived(moves, *slots):
        for slot in slots:
            moves[slot].wait_recv()

    def relayed(moves):
        for slot in (3, 4):
            moves[slot].wait_recv()
            moves[slot - 2].start()

    def sent(part, slot, moves, sbuf):
        sbuf[slot] = part.astype(BF16)
        moves[slot].start()

    def added(part, slot, moves, sbuf, rbuf):
        moves[slot - 2].wait_recv()
        sent(part + rbuf[slot - 2].astype(F32), slot, moves, sbuf)

    def settled(parts, moves, rbuf, out):
        for slot in (7, 8):
            part = parts[slot]
            for came in (slot - 2, slot - 4) + ((0,) if slot == 8 else ()):
                moves[came].wait_recv()
                part = part + rbuf[came].astype(F32)
            out[pl.ds((slot - AHEAD) * TILE, TILE), :] = part.astype(BF16)

    loads[1].wait()
    turned(q, qt)
    scores(7)
    scores(8)
    relayed(k_move)
    for slot in (5, 6, 0):
        v_move[slot].start()
    loads[3].wait()
    turned(g, gt)
    arrived(k_move, 5, 6)
    for slot in (5, 6, 3, 4):
        scores(slot)
    relayed(v_move)
    arrived(k_move, 0)
    scores(0)
    arrived(k_move, 1)
    scores(1)
    arrived(k_move, 2)
    scores(2)
    factors()

    v_part = {}
    for slot in (1, 2, 0, 5, 6):
        sent(value_part(slot), slot, v_home, sv)
    for slot in (3, 4, 7, 8):
        v_part[slot] = value_part(slot)
    dprobs(7)
    dprobs(8)
    arrived(v_move, 5, 6)
    for slot in (5, 6, 3, 4):
        dprobs(slot)
    arrived(v_move, 0)
    dprobs(0)
    added(v_part[3], 3, v_home, sv, rv)
    added(v_part[4], 4, v_home, sv, rv)
    arrived(v_move, 1)
    dprobs(1)
    arrived(v_move, 2)
    dprobs(2)
    deltas()

    k_part = {}
    for slot in (1, 2, 0, 5, 6):
        sent(key_part(slot), slot, k_home, sk)
    for slot in (3, 4, 7, 8):
        k_part[slot] = key_part(slot)
    query_part(0, dq_out)
    added(k_part[3], 3, k_home, sk, rk)
    added(k_part[4], 4, k_home, sk, rk)
    query_part(1, dq_out)
    settled(v_part, v_home, rv, dv_out)
    settled(k_part, k_home, rk, dk_out)

    for moves in (k_move, v_move, v_home, k_home):
        for move in moves:
            move.wait_send()


def shards(queries, keys, values, output_gradient, doc_tiles, doc_pads):
    rows, wide = queries.shape
    window = SLOTS * TILE
    both = 2 * (wide // HEAD) * TILE
    anywhere = pl.BlockSpec(memory_space=pl.ANY)
    vmem = pl.BlockSpec(memory_space=pltpu.VMEM)
    dma = pltpu.SemaphoreType.DMA
    operands = (doc_tiles, doc_pads, queries, keys, values, output_gradient)
    return pl.pallas_call(
        kernel,
        out_shape=(
            jax.ShapeDtypeStruct((rows, wide), BF16),
            jax.ShapeDtypeStruct(keys.shape, BF16),
            jax.ShapeDtypeStruct(values.shape, BF16),
        ),
        in_specs=[anywhere] * 6,
        out_specs=(vmem, vmem, vmem),
        scratch_shapes=[
            pltpu.SMEM(doc_tiles.shape, jnp.int32),
            pltpu.SMEM(doc_pads.shape, jnp.int32),
            pltpu.VMEM((rows, wide), BF16),
            pltpu.VMEM((rows, wide), BF16),
            pltpu.VMEM((HEAD, both), BF16),
            pltpu.VMEM((HEAD, both), BF16),
            pltpu.VMEM((window, HEAD), BF16),
            pltpu.VMEM((window, HEAD), BF16),
            pltpu.VMEM((HEAD, window), BF16),
            pltpu.VMEM((window, both), F32),
            pltpu.VMEM((window, both), BF16),
            pltpu.VMEM((16, both), F32),
            pltpu.VMEM((16, both), F32),
            pltpu.VMEM((16, both), F32),
            pltpu.VMEM((16, both), F32),
        ]
        + [pltpu.VMEM((AHEAD, TILE, HEAD), BF16)] * 4
        + [dma((6,))]
        + [dma((AHEAD,))] * 8,
        compiler_params=pltpu.CompilerParams(
            collective_id=0, has_side_effects=True, vmem_limit_bytes=48 * 1024 * 1024
        ),
        cost_estimate=pl.CostEstimate(flops=2_700_000_000, bytes_accessed=2_400_000, transcendentals=2_100_000),
        name="attention_backward",
    )(*[pltpu.with_memory_space_constraint(x, pltpu.HBM) for x in operands])


def solution(mesh):
    split = P(("ctx", "grp"), "tp")
    return jax.shard_map(
        shards,
        mesh=mesh,
        in_specs=(split, split, split, split, P(), P()),
        out_specs=(split, split, split),
        check_vma=False,
    )
```

```python
import math

import jax
import jax.numpy as jnp
from jax import lax
from jax.experimental import pallas as pl
from jax.experimental.pallas import tpu as pltpu
from jax.sharding import PartitionSpec as P

HEAD = 128
TILE = 128
SLOTS = 9
AHEAD = 7
NEG = -1e30
F32 = jnp.float32
BF16 = jnp.bfloat16


BACK = (4, 3, 3, 2, 2, 1, 1)
def kernel(
    tiles_hbm, pads_hbm, q_hbm, k_hbm, v_hbm, g_hbm,
    dq_out, dk_out, dv_out,
    tiles_ref, pads_ref, q, g, qt, gt, kw, vw, kt, e, p, m_ref, l_ref, f_ref, d_ref, sv, rv, sk, rk,
    local_sem, kss, krs, vss, vrs, svs, rvs, sks, rks,
):
    ctx, grp = lax.axis_index("ctx"), lax.axis_index("grp")
    nctx, ngrp = lax.axis_size("ctx"), lax.axis_size("grp")
    heads = q_hbm.shape[1] // HEAD
    cols = heads * TILE
    pairs = heads // 2
    scale = 1.0 / math.sqrt(HEAD)
    c2 = scale * math.log2(math.e)
    mine = ctx * ngrp + grp
    shards_all = nctx * ngrp

    def shard(distance):
        index = mine + distance
        return {"ctx": index // ngrp, "grp": index % ngrp}

    own = pl.ds(AHEAD * TILE, 2 * TILE)
    loads = [
        pltpu.make_async_copy(src, dst, local_sem.at[n])
        for n, (src, dst) in enumerate(
            (
                (k_hbm, kw.at[own]), (q_hbm, q), (v_hbm, vw.at[own]), (g_hbm, g),
                (tiles_hbm, tiles_ref), (pads_hbm, pads_ref),
            )
        )
    ]
    for load in loads:
        load.start()

    @pl.when(mine < 4)
    def _():
        kw[pl.ds(0, AHEAD * TILE)] = jnp.zeros((AHEAD * TILE, HEAD), BF16)
        vw[pl.ds(0, AHEAD * TILE)] = jnp.zeros((AHEAD * TILE, HEAD), BF16)

    @pl.when(mine >= shards_all - 4)
    def _():
        rv[...] = jnp.zeros(rv.shape, BF16)
        rk[...] = jnp.zeros(rk.shape, BF16)

    barrier = pltpu.get_barrier_semaphore()
    partners = jnp.int32(0)
    for distance in (1, 2):
        for to, there in ((distance, mine + distance < shards_all), (-distance, mine >= distance)):
            @pl.when(there)
            def _():
                pl.semaphore_signal(
                    barrier, inc=1, device_id=shard(to), device_id_type=pl.DeviceIdType.MESH
                )
            partners = partners + jnp.where(there, 1, 0)
    pl.semaphore_wait(barrier, partners)

    class Move:
        def __init__(self, src, dst, ssem, rsem, to, sends, receives):
            self.copy = pltpu.make_async_remote_copy(
                src_ref=src, dst_ref=dst, send_sem=ssem, recv_sem=rsem,
                device_id=shard(to), device_id_type=pl.DeviceIdType.MESH,
            )
            self.sends, self.receives = sends, receives

        def start(self):
            pl.when(self.sends)(self.copy.start)

        def wait_send(self):
            pl.when(self.sends)(self.copy.wait_send)

        def wait_recv(self):
            pl.when(self.receives)(self.copy.wait_recv)

    def ahead(win, ssem, rsem, dst):
        if BACK[dst] == 3:
            src, step, sends = dst + 2, 1, (mine >= 2) & (mine + 1 < shards_all)
        elif BACK[dst] == 1:
            src, step, sends = dst - 2, -1, mine >= 2
        elif BACK[dst] == 4:
            src, step, sends = 4, 2, (mine >= 2) & (mine + 2 < shards_all)
        else:
            src, step, sends = dst + 4, 2, mine + 2 < shards_all
        return Move(
            win.at[rows_of(src)], win.at[rows_of(dst)],
            ssem.at[dst], rsem.at[dst], step, sends, mine >= BACK[dst],
        )

    def ahead_last(win, ssem, rsem, dst):
        return Move(
            win.at[rows_of(dst + 2)], win.at[rows_of(dst)],
            ssem.at[dst - 2], rsem.at[dst], 1, mine == shards_all - 2, None,
        )

    def home(sbuf, rbuf, ssem, rsem, slot):
        if BACK[slot] == 3:
            to, sends = -1, mine >= 3
            receives = (mine >= 2) & (mine + 1 < shards_all)
        elif BACK[slot] == 1:
            to, sends, receives = 1, (mine >= 1) & (mine + 1 < shards_all), mine >= 2
        elif BACK[slot] == 4:
            to, sends = -2, mine >= 4
            receives = (mine >= 2) & (mine + 2 < shards_all)
        else:
            to, sends, receives = -2, mine >= 2, mine + 1 < shards_all
        return Move(
            sbuf.at[slot], rbuf.at[slot], ssem.at[slot], rsem.at[slot], to, sends, receives
        )

    def home_last(sbuf, rbuf, ssem, rsem, slot):
        return Move(
            sbuf.at[slot], rbuf.at[slot - 2], ssem.at[slot], rsem.at[slot - 2],
            -1, mine == shards_all - 1, None,
        )

    def rows_of(slot):
        return pl.ds(slot * TILE, TILE)

    k_move = [ahead(kw, kss, krs, dst) for dst in range(AHEAD)]
    v_move = [ahead(vw, vss, vrs, dst) for dst in range(AHEAD)]
    v_home = [home(sv, rv, svs, rvs, slot) for slot in range(AHEAD)]
    k_home = [home(sk, rk, sks, rks, slot) for slot in range(AHEAD)]
    k_move_last = {slot: ahead_last(kw, kss, krs, slot) for slot in (5, 6)}
    v_move_last = {slot: ahead_last(vw, vss, vrs, slot) for slot in (5, 6)}
    v_home_last = {slot: home_last(sv, rv, svs, rvs, slot) for slot in (5, 6)}
    k_home_last = {slot: home_last(sk, rk, sks, rks, slot) for slot in (5, 6)}

    def launched(moves, last, *slots):
        for slot in slots:
            moves[slot].start()
            if slot in (3, 4):
                last[slot + 2].start()

    loads[0].wait()
    launched(k_move, k_move_last, 3, 4)
    loads[2].wait()

    loads[4].wait()
    loads[5].wait()
    first = [jnp.int32(0), jnp.int32(0)]
    stop = [jnp.int32(0), jnp.int32(0)]
    at = jnp.int32(0)
    for j in range(tiles_ref.shape[0]):
        after = at + tiles_ref[j]
        end = after * TILE - pads_ref[j]
        for i in range(2):
            tile = 2 * mine + i
            inside = (at <= tile) & (tile < after)
            first[i] = jnp.where(inside, at, first[i])
            stop[i] = jnp.where(inside, end, stop[i])
        at = after

    def cols_of(i, c):
        return pl.ds(pl.multiple_of(i * cols + c * 2 * TILE, TILE), 2 * TILE)

    def two_heads(ref, i, c):
        at_row = pl.ds(i * TILE, TILE)
        return jnp.concatenate(
            [
                ref[at_row, pl.ds(pl.multiple_of((2 * c + n) * HEAD, HEAD), HEAD)]
                for n in range(2)
            ],
            axis=0,
        )

    def tiles_of(slot):
        return [i for i in range(2) if i <= slot <= AHEAD + i]

    def over_pairs(body, init=0):
        return lax.fori_loop(0, pairs, body, init, unroll=True)

    def scores(slot):
        def step(c, carry):
            key = kw[rows_of(slot)]
            for i in tiles_of(slot):
                s = jnp.dot(key, qt[:, cols_of(i, c)], preferred_element_type=F32)
                if slot == AHEAD + i:
                    row = lax.broadcasted_iota(jnp.int32, s.shape, 0)
                    col = lax.broadcasted_iota(jnp.int32, s.shape, 1)
                    s = jnp.where(row <= (col & (TILE - 1)), s, NEG)
                top = jnp.max(s, axis=0, keepdims=True) * c2
                w = jnp.exp2(s * c2 - top)
                e[rows_of(slot), cols_of(i, c)] = w
                m_ref[pl.ds(slot, 1), cols_of(i, c)] = top
                l_ref[pl.ds(slot, 1), cols_of(i, c)] = jnp.sum(w, axis=0, keepdims=True)
            return carry

        over_pairs(step)
        kt[:, rows_of(slot)] = jnp.transpose(kw[rows_of(slot)])

    def factors():
        for i in range(2):
            part = pl.ds(i * cols, cols)
            shape = (16, cols)
            row = lax.broadcasted_iota(jnp.int32, shape, 0)
            token = lax.broadcasted_iota(jnp.int32, shape, 1) & (TILE - 1)
            tile = 2 * mine + i
            valid = (row >= i) & (row <= AHEAD + i) & (row + (2 * mine - AHEAD) >= first[i])
            tops = jnp.where(valid, m_ref[:, part], NEG)
            w = jnp.exp2(tops - jnp.max(tops, axis=0, keepdims=True))
            total = jnp.sum(w * jnp.where(valid, l_ref[:, part], 0.0), axis=0, keepdims=True)
            live = token < stop[i] - tile * TILE
            f_ref[:, part] = jnp.where(live, w / total, 0.0)

    def value_part(slot):
        def step(c, acc):
            for i in tiles_of(slot):
                w = e[rows_of(slot), cols_of(i, c)] * f_ref[pl.ds(slot, 1), cols_of(i, c)]
                w = w.astype(BF16)
                p[rows_of(slot), cols_of(i, c)] = w
                acc = acc + jnp.dot(w, two_heads(g, i, c), preferred_element_type=F32)
            return acc

        return over_pairs(step, jnp.zeros((TILE, HEAD), F32))

    def dprobs(slot):
        def step(c, carry):
            value = vw[rows_of(slot)]
            for i in tiles_of(slot):
                d = jnp.dot(value, gt[:, cols_of(i, c)], preferred_element_type=F32)
                e[rows_of(slot), cols_of(i, c)] = d
                d = d * p[rows_of(slot), cols_of(i, c)].astype(F32)
                d_ref[pl.ds(slot, 1), cols_of(i, c)] = jnp.sum(d, axis=0, keepdims=True)
            return carry

        over_pairs(step)

    def deltas():
        for i in range(2):
            part = pl.ds(i * cols, cols)
            row = lax.broadcasted_iota(jnp.int32, (16, cols), 0)
            terms = jnp.where((row >= i) & (row <= AHEAD + i), d_ref[:, part], 0.0)
            f_ref[:, part] = jnp.broadcast_to(jnp.sum(terms, axis=0, keepdims=True), (16, cols))

    def key_part(slot):
        def step(c, acc):
            for i in tiles_of(slot):
                d = e[rows_of(slot), cols_of(i, c)] - f_ref[pl.ds(0, 1), cols_of(i, c)]
                d = (p[rows_of(slot), cols_of(i, c)].astype(F32) * d).astype(BF16)
                p[rows_of(slot), cols_of(i, c)] = d
                acc = acc + jnp.dot(d, two_heads(q, i, c), preferred_element_type=F32)
            return acc

        return over_pairs(step, jnp.zeros((TILE, HEAD), F32)) * scale

    def query_part(i, dq):
        window = pl.ds(i * TILE, (SLOTS - 1) * TILE)

        def step(c, carry):
            t = jnp.dot(kt[:, window], p[window, cols_of(i, c)], preferred_element_type=F32) * scale
            for n in range(2):
                head = pl.ds(pl.multiple_of((2 * c + n) * HEAD, HEAD), HEAD)
                t_head = t[:, n * TILE : (n + 1) * TILE]
                dq[pl.ds(i * TILE, TILE), head] = jnp.transpose(t_head).astype(BF16)
            return carry

        over_pairs(step)

    def turned(ref, out):
        def step(c, carry):
            for i in range(2):
                for n in range(2):
                    head = pl.ds(pl.multiple_of((2 * c + n) * HEAD, HEAD), HEAD)
                    at_col = pl.ds(pl.multiple_of(i * cols + (2 * c + n) * TILE, TILE), TILE)
                    out[:, at_col] = jnp.transpose(ref[pl.ds(i * TILE, TILE), head])
            return carry

        over_pairs(step)

    def arrived(moves, *slots):
        for slot in slots:
            moves[slot].wait_recv()

    def relayed(moves):
        for slot in (3, 4):
            moves[slot].wait_recv()
            moves[slot - 2].start()
            moves[slot + 2].start()
        moves[0].start()

    def sent(part, slot, moves, last, sbuf):
        sbuf[slot] = part.astype(BF16)
        moves[slot].start()
        if slot in (5, 6):
            last[slot].start()

    def added(part, slot, moves, last, sbuf, rbuf):
        for came in (1, 5) if slot == 3 else (2, 6, 0):
            moves[came].wait_recv()
            part = part + rbuf[came].astype(F32)
        sent(part, slot, moves, last, sbuf)

    def settled(parts, moves, rbuf, out):
        for slot in (7, 8):
            moves[slot - 4].wait_recv()
            part = parts[slot] + rbuf[slot - 4].astype(F32)
            out[rows_of(slot - AHEAD), :] = part.astype(BF16)

    loads[1].wait()
    turned(q, qt)
    scores(7)
    scores(8)
    launched(v_move, v_move_last, 3, 4)
    relayed(k_move)
    loads[3].wait()
    turned(g, gt)
    for slot in (3, 4):
        scores(slot)
    relayed(v_move)
    for slot in (1, 5, 2, 6, 0):
        arrived(k_move, slot)
        scores(slot)
    factors()

    v_part = {}
    for slot in (1, 5, 2, 6, 0):
        sent(value_part(slot), slot, v_home, v_home_last, sv)
    for slot in (3, 4, 7, 8):
        v_part[slot] = value_part(slot)
    for slot in (7, 8, 3, 4):
        dprobs(slot)
    for slot in (1, 5, 2, 6, 0):
        arrived(v_move, slot)
        dprobs(slot)
    deltas()

    k_part = {}
    for slot in (1, 5, 2, 6, 0):
        sent(key_part(slot), slot, k_home, k_home_last, sk)
    for slot in (3, 4):
        added(v_part[slot], slot, v_home, v_home_last, sv, rv)
    for slot in (3, 4, 7, 8):
        k_part[slot] = key_part(slot)
    query_part(0, dq_out)
    added(k_part[3], 3, k_home, k_home_last, sk, rk)
    added(k_part[4], 4, k_home, k_home_last, sk, rk)
    query_part(1, dq_out)
    settled(v_part, v_home, rv, dv_out)
    settled(k_part, k_home, rk, dk_out)

    for moves in (k_move, v_move, v_home, k_home):
        for move in moves:
            move.wait_send()
    for moves in (k_move_last, v_move_last, v_home_last, k_home_last):
        for move in moves.values():
            move.wait_send()


def store(dq, dk, dv, dq_out, dk_out, dv_out, sem):
    moves = [
        pltpu.make_async_copy(src, dst, sem.at[n])
        for n, (src, dst) in enumerate(((dq, dq_out), (dk, dk_out), (dv, dv_out)))
    ]
    for move in moves:
        move.start()
    for move in moves:
        move.wait()


def shards(queries, keys, values, output_gradient, doc_tiles, doc_pads):
    rows, wide = queries.shape
    window = SLOTS * TILE
    both = 2 * (wide // HEAD) * TILE
    anywhere = pl.BlockSpec(memory_space=pl.ANY)
    vmem = pl.BlockSpec(memory_space=pltpu.VMEM)
    dma = pltpu.SemaphoreType.DMA
    operands = (doc_tiles, doc_pads, queries, keys, values, output_gradient)
    shapes = tuple(jax.ShapeDtypeStruct(x.shape, BF16) for x in (queries, keys, values))
    grads = pl.pallas_call(
        kernel,
        out_shape=shapes,
        in_specs=[anywhere] * 6,
        out_specs=(vmem, vmem, vmem),
        scratch_shapes=[
            pltpu.SMEM(doc_tiles.shape, jnp.int32),
            pltpu.SMEM(doc_pads.shape, jnp.int32),
            pltpu.VMEM((rows, wide), BF16),
            pltpu.VMEM((rows, wide), BF16),
            pltpu.VMEM((HEAD, both), BF16),
            pltpu.VMEM((HEAD, both), BF16),
            pltpu.VMEM((window, HEAD), BF16),
            pltpu.VMEM((window, HEAD), BF16),
            pltpu.VMEM((HEAD, window), BF16),
            pltpu.VMEM((window, both), F32),
            pltpu.VMEM((window, both), BF16),
            pltpu.VMEM((16, both), F32),
            pltpu.VMEM((16, both), F32),
            pltpu.VMEM((16, both), F32),
            pltpu.VMEM((16, both), F32),
        ]
        + [pltpu.VMEM((AHEAD, TILE, HEAD), BF16)] * 4
        + [dma((6,))]
        + [dma((AHEAD,))] * 8,
        compiler_params=pltpu.CompilerParams(
            collective_id=0, has_side_effects=True, vmem_limit_bytes=48 * 1024 * 1024
        ),
        cost_estimate=pl.CostEstimate(flops=2_700_000_000, bytes_accessed=2_400_000, transcendentals=2_100_000),
        name="attention_backward",
    )(*[pltpu.with_memory_space_constraint(x, pltpu.HBM) for x in operands])
    return pl.pallas_call(
        store,
        out_shape=shapes,
        in_specs=[vmem] * 3,
        out_specs=(anywhere,) * 3,
        scratch_shapes=[dma((3,))],
        name="store_gradients",
    )(*[pltpu.with_memory_space_constraint(x, pltpu.VMEM) for x in grads])


def solution(mesh):
    split = P(("ctx", "grp"), "tp")
    return jax.shard_map(
        shards,
        mesh=mesh,
        in_specs=(split, split, split, split, P(), P()),
        out_specs=(split, split, split),
        check_vma=False,
    )
```

```python
import math

import jax
import jax.numpy as jnp
from jax import lax
from jax.experimental import pallas as pl
from jax.experimental.pallas import tpu as pltpu
from jax.sharding import PartitionSpec as P

HEAD = 128
TILE = 128
SLOTS = 9
AHEAD = 7
NEG = -1e30
F32 = jnp.float32
BF16 = jnp.bfloat16


BACK = (4, 3, 3, 2, 2, 1, 1)
EARLY = (3, 4, 7, 8)
def kernel(
    tiles_hbm, pads_hbm, q_hbm, k_hbm, v_hbm, g_hbm,
    dq_out, dk_out, dv_out,
    tiles_ref, pads_ref, q, g, qt, gt, kw, vw, kt, e, dp, p, m_ref, l_ref, f_ref, d_ref, sv, rv, sk, rk,
    local_sem, kss, krs, vss, vrs, svs, rvs, sks, rks,
):
    ctx, grp = lax.axis_index("ctx"), lax.axis_index("grp")
    nctx, ngrp = lax.axis_size("ctx"), lax.axis_size("grp")
    heads = q_hbm.shape[1] // HEAD
    cols = heads * TILE
    pairs = heads // 2
    scale = 1.0 / math.sqrt(HEAD)
    c2 = scale * math.log2(math.e)
    mine = ctx * ngrp + grp
    shards_all = nctx * ngrp

    def shard(distance):
        index = mine + distance
        return {"ctx": index // ngrp, "grp": index % ngrp}

    own = pl.ds(AHEAD * TILE, 2 * TILE)
    loads = [
        pltpu.make_async_copy(src, dst, local_sem.at[n])
        for n, (src, dst) in enumerate(
            (
                (k_hbm, kw.at[own]), (q_hbm, q), (v_hbm, vw.at[own]), (g_hbm, g),
                (tiles_hbm, tiles_ref), (pads_hbm, pads_ref),
            )
        )
    ]
    for load in loads:
        load.start()

    @pl.when(mine < 4)
    def _():
        kw[pl.ds(0, AHEAD * TILE)] = jnp.zeros((AHEAD * TILE, HEAD), BF16)
        vw[pl.ds(0, AHEAD * TILE)] = jnp.zeros((AHEAD * TILE, HEAD), BF16)

    @pl.when(mine >= shards_all - 4)
    def _():
        rv[...] = jnp.zeros(rv.shape, BF16)
        rk[...] = jnp.zeros(rk.shape, BF16)

    barrier = pltpu.get_barrier_semaphore()
    partners = jnp.int32(0)
    for distance in (1, 2):
        for to, there in ((distance, mine + distance < shards_all), (-distance, mine >= distance)):
            @pl.when(there)
            def _():
                pl.semaphore_signal(
                    barrier, inc=1, device_id=shard(to), device_id_type=pl.DeviceIdType.MESH
                )
            partners = partners + jnp.where(there, 1, 0)
    pl.semaphore_wait(barrier, partners)

    class Move:
        def __init__(self, src, dst, ssem, rsem, to, sends, receives):
            self.copy = pltpu.make_async_remote_copy(
                src_ref=src, dst_ref=dst, send_sem=ssem, recv_sem=rsem,
                device_id=shard(to), device_id_type=pl.DeviceIdType.MESH,
            )
            self.sends, self.receives = sends, receives

        def start(self):
            pl.when(self.sends)(self.copy.start)

        def wait_send(self):
            pl.when(self.sends)(self.copy.wait_send)

        def wait_recv(self):
            pl.when(self.receives)(self.copy.wait_recv)

    def ahead(win, ssem, rsem, dst):
        if BACK[dst] == 3:
            src, step, sends = dst + 2, 1, (mine >= 2) & (mine + 1 < shards_all)
        elif BACK[dst] == 1:
            src, step, sends = dst - 2, -1, mine >= 2
        elif BACK[dst] == 4:
            src, step, sends = 4, 2, (mine >= 2) & (mine + 2 < shards_all)
        else:
            src, step, sends = dst + 4, 2, mine + 2 < shards_all
        return Move(
            win.at[rows_of(src)], win.at[rows_of(dst)],
            ssem.at[dst], rsem.at[dst], step, sends, mine >= BACK[dst],
        )

    def ahead_last(win, ssem, rsem, dst):
        return Move(
            win.at[rows_of(dst + 2)], win.at[rows_of(dst)],
            ssem.at[dst - 2], rsem.at[dst], 1, mine == shards_all - 2, None,
        )

    def home(sbuf, rbuf, ssem, rsem, slot):
        if BACK[slot] == 3:
            to, sends = -1, mine >= 3
            receives = (mine >= 2) & (mine + 1 < shards_all)
        elif BACK[slot] == 1:
            to, sends, receives = 1, (mine >= 1) & (mine + 1 < shards_all), mine >= 2
        elif BACK[slot] == 4:
            to, sends = -2, mine >= 4
            receives = (mine >= 2) & (mine + 2 < shards_all)
        else:
            to, sends, receives = -2, mine >= 2, mine + 1 < shards_all
        return Move(
            sbuf.at[slot], rbuf.at[slot], ssem.at[slot], rsem.at[slot], to, sends, receives
        )

    def home_last(sbuf, rbuf, ssem, rsem, slot):
        return Move(
            sbuf.at[slot], rbuf.at[slot - 2], ssem.at[slot], rsem.at[slot - 2],
            -1, mine == shards_all - 1, None,
        )

    def rows_of(slot):
        return pl.ds(slot * TILE, TILE)

    k_move = [ahead(kw, kss, krs, dst) for dst in range(AHEAD)]
    v_move = [ahead(vw, vss, vrs, dst) for dst in range(AHEAD)]
    v_home = [home(sv, rv, svs, rvs, slot) for slot in range(AHEAD)]
    k_home = [home(sk, rk, sks, rks, slot) for slot in range(AHEAD)]
    k_move_last = {slot: ahead_last(kw, kss, krs, slot) for slot in (5, 6)}
    v_move_last = {slot: ahead_last(vw, vss, vrs, slot) for slot in (5, 6)}
    v_home_last = {slot: home_last(sv, rv, svs, rvs, slot) for slot in (5, 6)}
    k_home_last = {slot: home_last(sk, rk, sks, rks, slot) for slot in (5, 6)}

    def launched(moves, last, *slots):
        for slot in slots:
            moves[slot].start()
            if slot in (3, 4):
                last[slot + 2].start()

    loads[0].wait()
    launched(k_move, k_move_last, 4, 3)
    loads[2].wait()

    loads[4].wait()
    loads[5].wait()
    first = [jnp.int32(0), jnp.int32(0)]
    stop = [jnp.int32(0), jnp.int32(0)]
    at = jnp.int32(0)
    for j in range(tiles_ref.shape[0]):
        after = at + tiles_ref[j]
        end = after * TILE - pads_ref[j]
        for i in range(2):
            tile = 2 * mine + i
            inside = (at <= tile) & (tile < after)
            first[i] = jnp.where(inside, at, first[i])
            stop[i] = jnp.where(inside, end, stop[i])
        at = after

    def cols_of(i, c):
        return pl.ds(pl.multiple_of(i * cols + c * 2 * TILE, TILE), 2 * TILE)

    def two_heads(ref, i, c):
        at_row = pl.ds(i * TILE, TILE)
        return jnp.concatenate(
            [
                ref[at_row, pl.ds(pl.multiple_of((2 * c + n) * HEAD, HEAD), HEAD)]
                for n in range(2)
            ],
            axis=0,
        )

    def tiles_of(slot):
        return [i for i in range(2) if i <= slot <= AHEAD + i]

    def over_pairs(body, init=0):
        return lax.fori_loop(0, pairs, body, init, unroll=True)

    def scores(slot):
        def step(c, carry):
            key = kw[rows_of(slot)]
            for i in tiles_of(slot):
                s = jnp.dot(key, qt[:, cols_of(i, c)], preferred_element_type=F32)
                if slot == AHEAD + i:
                    row = lax.broadcasted_iota(jnp.int32, s.shape, 0)
                    col = lax.broadcasted_iota(jnp.int32, s.shape, 1)
                    s = jnp.where(row <= (col & (TILE - 1)), s, NEG)
                top = jnp.max(s, axis=0, keepdims=True) * c2
                w = jnp.exp2(s * c2 - top)
                e[rows_of(slot), cols_of(i, c)] = w
                m_ref[pl.ds(slot, 1), cols_of(i, c)] = top
                l_ref[pl.ds(slot, 1), cols_of(i, c)] = jnp.sum(w, axis=0, keepdims=True)
            return carry

        over_pairs(step)
        kt[:, rows_of(slot)] = jnp.transpose(kw[rows_of(slot)])

    def factors():
        for i in range(2):
            part = pl.ds(i * cols, cols)
            shape = (16, cols)
            row = lax.broadcasted_iota(jnp.int32, shape, 0)
            token = lax.broadcasted_iota(jnp.int32, shape, 1) & (TILE - 1)
            tile = 2 * mine + i
            valid = (row >= i) & (row <= AHEAD + i) & (row + (2 * mine - AHEAD) >= first[i])
            tops = jnp.where(valid, m_ref[:, part], NEG)
            w = jnp.exp2(tops - jnp.max(tops, axis=0, keepdims=True))
            total = jnp.sum(w * jnp.where(valid, l_ref[:, part], 0.0), axis=0, keepdims=True)
            live = token < stop[i] - tile * TILE
            f_ref[:, part] = jnp.where(live, w / total, 0.0)

    def value_part(slot):
        def step(c, acc):
            for i in tiles_of(slot):
                w = e[rows_of(slot), cols_of(i, c)] * f_ref[pl.ds(slot, 1), cols_of(i, c)]
                w = w.astype(BF16)
                p[rows_of(slot), cols_of(i, c)] = w
                acc = acc + jnp.dot(w, two_heads(g, i, c), preferred_element_type=F32)
                if slot in EARLY:
                    d = dp[rows_of(slot), cols_of(i, c)] * w.astype(F32)
                    d_ref[pl.ds(slot, 1), cols_of(i, c)] = jnp.sum(d, axis=0, keepdims=True)
            return acc

        return over_pairs(step, jnp.zeros((TILE, HEAD), F32))

    def dprobs_raw(slot):
        def step(c, carry):
            value = vw[rows_of(slot)]
            for i in tiles_of(slot):
                dp[rows_of(slot), cols_of(i, c)] = jnp.dot(
                    value, gt[:, cols_of(i, c)], preferred_element_type=F32
                )
            return carry

        over_pairs(step)

    def dprobs(slot):
        def step(c, carry):
            value = vw[rows_of(slot)]
            for i in tiles_of(slot):
                d = jnp.dot(value, gt[:, cols_of(i, c)], preferred_element_type=F32)
                dp[rows_of(slot), cols_of(i, c)] = d
                d = d * p[rows_of(slot), cols_of(i, c)].astype(F32)
                d_ref[pl.ds(slot, 1), cols_of(i, c)] = jnp.sum(d, axis=0, keepdims=True)
            return carry

        over_pairs(step)

    def deltas():
        for i in range(2):
            part = pl.ds(i * cols, cols)
            row = lax.broadcasted_iota(jnp.int32, (16, cols), 0)
            terms = jnp.where((row >= i) & (row <= AHEAD + i), d_ref[:, part], 0.0)
            f_ref[:, part] = jnp.broadcast_to(jnp.sum(terms, axis=0, keepdims=True), (16, cols))

    def key_part(slot):
        def step(c, acc):
            for i in tiles_of(slot):
                d = dp[rows_of(slot), cols_of(i, c)] - f_ref[pl.ds(0, 1), cols_of(i, c)]
                d = (p[rows_of(slot), cols_of(i, c)].astype(F32) * d).astype(BF16)
                p[rows_of(slot), cols_of(i, c)] = d
                acc = acc + jnp.dot(d, two_heads(q, i, c), preferred_element_type=F32)
            return acc

        return over_pairs(step, jnp.zeros((TILE, HEAD), F32)) * scale

    def query_part(i, dq):
        window = pl.ds(i * TILE, (SLOTS - 1) * TILE)

        def step(c, carry):
            t = jnp.dot(kt[:, window], p[window, cols_of(i, c)], preferred_element_type=F32) * scale
            for n in range(2):
                head = pl.ds(pl.multiple_of((2 * c + n) * HEAD, HEAD), HEAD)
                t_head = t[:, n * TILE : (n + 1) * TILE]
                dq[pl.ds(i * TILE, TILE), head] = jnp.transpose(t_head).astype(BF16)
            return carry

        over_pairs(step)

    def turned(ref, out):
        def step(c, carry):
            for i in range(2):
                for n in range(2):
                    head = pl.ds(pl.multiple_of((2 * c + n) * HEAD, HEAD), HEAD)
                    at_col = pl.ds(pl.multiple_of(i * cols + (2 * c + n) * TILE, TILE), TILE)
                    out[:, at_col] = jnp.transpose(ref[pl.ds(i * TILE, TILE), head])
            return carry

        over_pairs(step)

    def arrived(moves, *slots):
        for slot in slots:
            moves[slot].wait_recv()

    def relayed(moves):
        for slot, onward in ((4, (0, 2, 6)), (3, (1, 5))):
            moves[slot].wait_recv()
            for dst in onward:
                moves[dst].start()

    def sent(part, slot, moves, last, sbuf):
        sbuf[slot] = part.astype(BF16)
        moves[slot].start()
        if slot in (5, 6):
            last[slot].start()

    def added(part, slot, moves, last, sbuf, rbuf):
        for came in (1, 5) if slot == 3 else (2, 6, 0):
            moves[came].wait_recv()
            part = part + rbuf[came].astype(F32)
        sent(part, slot, moves, last, sbuf)

    def settled(parts, moves, rbuf, out):
        for slot in (7, 8):
            moves[slot - 4].wait_recv()
            part = parts[slot] + rbuf[slot - 4].astype(F32)
            out[rows_of(slot - AHEAD), :] = part.astype(BF16)

    loads[1].wait()
    turned(q, qt)
    launched(v_move, v_move_last, 4, 3)
    scores(7)
    scores(8)
    relayed(k_move)
    loads[3].wait()
    turned(g, gt)
    for slot in (3, 4):
        scores(slot)
    for slot in (7, 8):
        dprobs_raw(slot)
    relayed(v_move)
    for slot in (3, 4):
        dprobs_raw(slot)
    for slot in (2, 6, 0, 1, 5):
        arrived(k_move, slot)
        scores(slot)
    factors()

    v_part = {}
    for slot in (0, 2, 6, 1, 5):
        sent(value_part(slot), slot, v_home, v_home_last, sv)
    for slot in (3, 4, 7, 8):
        v_part[slot] = value_part(slot)
    for slot in (2, 6, 0, 1, 5):
        arrived(v_move, slot)
        dprobs(slot)
    deltas()

    k_part = {}
    for slot in (0, 2, 6, 1, 5):
        sent(key_part(slot), slot, k_home, k_home_last, sk)
    for slot in (4, 3):
        added(v_part[slot], slot, v_home, v_home_last, sv, rv)
    for slot in (3, 4, 7, 8):
        k_part[slot] = key_part(slot)
    query_part(0, dq_out)
    added(k_part[4], 4, k_home, k_home_last, sk, rk)
    added(k_part[3], 3, k_home, k_home_last, sk, rk)
    query_part(1, dq_out)
    settled(v_part, v_home, rv, dv_out)
    settled(k_part, k_home, rk, dk_out)

    for moves in (k_move, v_move, v_home, k_home):
        for move in moves:
            move.wait_send()
    for moves in (k_move_last, v_move_last, v_home_last, k_home_last):
        for move in moves.values():
            move.wait_send()


def store(dq, dk, dv, dq_out, dk_out, dv_out, sem):
    moves = [
        pltpu.make_async_copy(src, dst, sem.at[n])
        for n, (src, dst) in enumerate(((dq, dq_out), (dk, dk_out), (dv, dv_out)))
    ]
    for move in moves:
        move.start()
    for move in moves:
        move.wait()


def shards(queries, keys, values, output_gradient, doc_tiles, doc_pads):
    rows, wide = queries.shape
    window = SLOTS * TILE
    both = 2 * (wide // HEAD) * TILE
    anywhere = pl.BlockSpec(memory_space=pl.ANY)
    vmem = pl.BlockSpec(memory_space=pltpu.VMEM)
    dma = pltpu.SemaphoreType.DMA
    operands = (doc_tiles, doc_pads, queries, keys, values, output_gradient)
    shapes = tuple(jax.ShapeDtypeStruct(x.shape, BF16) for x in (queries, keys, values))
    grads = pl.pallas_call(
        kernel,
        out_shape=shapes,
        in_specs=[anywhere] * 6,
        out_specs=(vmem, vmem, vmem),
        scratch_shapes=[
            pltpu.SMEM(doc_tiles.shape, jnp.int32),
            pltpu.SMEM(doc_pads.shape, jnp.int32),
            pltpu.VMEM((rows, wide), BF16),
            pltpu.VMEM((rows, wide), BF16),
            pltpu.VMEM((HEAD, both), BF16),
            pltpu.VMEM((HEAD, both), BF16),
            pltpu.VMEM((window, HEAD), BF16),
            pltpu.VMEM((window, HEAD), BF16),
            pltpu.VMEM((HEAD, window), BF16),
            pltpu.VMEM((window, both), F32),
            pltpu.VMEM((window, both), F32),
            pltpu.VMEM((window, both), BF16),
            pltpu.VMEM((16, both), F32),
            pltpu.VMEM((16, both), F32),
            pltpu.VMEM((16, both), F32),
            pltpu.VMEM((16, both), F32),
        ]
        + [pltpu.VMEM((AHEAD, TILE, HEAD), BF16)] * 4
        + [dma((6,))]
        + [dma((AHEAD,))] * 8,
        compiler_params=pltpu.CompilerParams(
            collective_id=0, has_side_effects=True, vmem_limit_bytes=48 * 1024 * 1024
        ),
        cost_estimate=pl.CostEstimate(flops=2_700_000_000, bytes_accessed=2_400_000, transcendentals=2_100_000),
        name="attention_backward",
    )(*[pltpu.with_memory_space_constraint(x, pltpu.HBM) for x in operands])
    return pl.pallas_call(
        store,
        out_shape=shapes,
        in_specs=[vmem] * 3,
        out_specs=(anywhere,) * 3,
        scratch_shapes=[dma((3,))],
        name="store_gradients",
    )(*[pltpu.with_memory_space_constraint(x, pltpu.VMEM) for x in grads])


def solution(mesh):
    split = P(("ctx", "grp"), "tp")
    return jax.shard_map(
        shards,
        mesh=mesh,
        in_specs=(split, split, split, split, P(), P()),
        out_specs=(split, split, split),
        check_vma=False,
    )
```

```python
import math

import jax
import jax.numpy as jnp
from jax import lax
from jax.experimental import pallas as pl
from jax.experimental.pallas import tpu as pltpu
from jax.sharding import PartitionSpec as P

HEAD = 128
TILE = 128
SLOTS = 9
AHEAD = 7
NEG = -1e30
F32 = jnp.float32
BF16 = jnp.bfloat16


BACK = (4, 3, 3, 2, 2, 1, 1)
EARLY = (3, 4, 7, 8)
def kernel(
    tiles_hbm, pads_hbm, q_hbm, k_hbm, v_hbm, g_hbm,
    dq_out, dk_out, dv_out,
    tiles_ref, pads_ref, q, g, qt, gt, kw, vw, kt, e, dp, p, m_ref, l_ref, f_ref, d_ref, sv, rv, sk, rk,
    local_sem, kss, krs, vss, vrs, svs, rvs, sks, rks,
):
    ctx, grp = lax.axis_index("ctx"), lax.axis_index("grp")
    nctx, ngrp = lax.axis_size("ctx"), lax.axis_size("grp")
    heads = q_hbm.shape[1] // HEAD
    cols = heads * TILE
    pairs = heads // 2
    scale = 1.0 / math.sqrt(HEAD)
    c2 = scale * math.log2(math.e)
    mine = ctx * ngrp + grp
    shards_all = nctx * ngrp

    def shard(distance):
        index = mine + distance
        return {"ctx": index // ngrp, "grp": index % ngrp}

    own = pl.ds(AHEAD * TILE, 2 * TILE)
    loads = [
        pltpu.make_async_copy(src, dst, local_sem.at[n])
        for n, (src, dst) in enumerate(
            (
                (k_hbm, kw.at[own]), (q_hbm, q), (v_hbm, vw.at[own]), (g_hbm, g),
                (tiles_hbm, tiles_ref), (pads_hbm, pads_ref),
            )
        )
    ]
    for load in loads:
        load.start()

    @pl.when(mine < 4)
    def _():
        kw[pl.ds(0, AHEAD * TILE)] = jnp.zeros((AHEAD * TILE, HEAD), BF16)
        vw[pl.ds(0, AHEAD * TILE)] = jnp.zeros((AHEAD * TILE, HEAD), BF16)

    @pl.when(mine >= shards_all - 4)
    def _():
        rv[...] = jnp.zeros(rv.shape, BF16)
        rk[...] = jnp.zeros(rk.shape, BF16)

    barrier = pltpu.get_barrier_semaphore()
    partners = jnp.int32(0)
    for distance in (1, 2):
        for to, there in ((distance, mine + distance < shards_all), (-distance, mine >= distance)):
            @pl.when(there)
            def _():
                pl.semaphore_signal(
                    barrier, inc=1, device_id=shard(to), device_id_type=pl.DeviceIdType.MESH
                )
            partners = partners + jnp.where(there, 1, 0)
    pl.semaphore_wait(barrier, partners)

    class Move:
        def __init__(self, src, dst, ssem, rsem, to, sends, receives):
            self.copy = pltpu.make_async_remote_copy(
                src_ref=src, dst_ref=dst, send_sem=ssem, recv_sem=rsem,
                device_id=shard(to), device_id_type=pl.DeviceIdType.MESH,
            )
            self.sends, self.receives = sends, receives

        def start(self):
            pl.when(self.sends)(self.copy.start)

        def wait_send(self):
            pl.when(self.sends)(self.copy.wait_send)

        def wait_recv(self):
            pl.when(self.receives)(self.copy.wait_recv)

    def ahead(win, ssem, rsem, dst):
        if BACK[dst] == 3:
            src, step, sends = dst + 2, 1, (mine >= 2) & (mine + 1 < shards_all)
        elif BACK[dst] == 1:
            src, step, sends = dst - 2, -1, mine >= 2
        elif BACK[dst] == 4:
            src, step, sends = 4, 2, (mine >= 2) & (mine + 2 < shards_all)
        else:
            src, step, sends = dst + 4, 2, mine + 2 < shards_all
        return Move(
            win.at[rows_of(src)], win.at[rows_of(dst)],
            ssem.at[dst], rsem.at[dst], step, sends, mine >= BACK[dst],
        )

    def ahead_last(win, ssem, rsem, dst):
        return Move(
            win.at[rows_of(dst + 2)], win.at[rows_of(dst)],
            ssem.at[dst - 2], rsem.at[dst], 1, mine == shards_all - 2, None,
        )

    def home(sbuf, rbuf, ssem, rsem, slot):
        if BACK[slot] == 3:
            to, sends = -1, mine >= 3
            receives = (mine >= 2) & (mine + 1 < shards_all)
        elif BACK[slot] == 1:
            to, sends, receives = 1, (mine >= 1) & (mine + 1 < shards_all), mine >= 2
        elif BACK[slot] == 4:
            to, sends = -2, mine >= 4
            receives = (mine >= 2) & (mine + 2 < shards_all)
        else:
            to, sends, receives = -2, mine >= 2, mine + 1 < shards_all
        return Move(
            sbuf.at[slot], rbuf.at[slot], ssem.at[slot], rsem.at[slot], to, sends, receives
        )

    def home_last(sbuf, rbuf, ssem, rsem, slot):
        return Move(
            sbuf.at[slot], rbuf.at[slot - 2], ssem.at[slot], rsem.at[slot - 2],
            -1, mine == shards_all - 1, None,
        )

    def rows_of(slot):
        return pl.ds(slot * TILE, TILE)

    k_move = [ahead(kw, kss, krs, dst) for dst in range(AHEAD)]
    v_move = [ahead(vw, vss, vrs, dst) for dst in range(AHEAD)]
    v_home = [home(sv, rv, svs, rvs, slot) for slot in range(AHEAD)]
    k_home = [home(sk, rk, sks, rks, slot) for slot in range(AHEAD)]
    k_move_last = {slot: ahead_last(kw, kss, krs, slot) for slot in (5, 6)}
    v_move_last = {slot: ahead_last(vw, vss, vrs, slot) for slot in (5, 6)}
    v_home_last = {slot: home_last(sv, rv, svs, rvs, slot) for slot in (5, 6)}
    k_home_last = {slot: home_last(sk, rk, sks, rks, slot) for slot in (5, 6)}

    def launched(moves, last, *slots):
        for slot in slots:
            moves[slot].start()
            if slot in (3, 4):
                last[slot + 2].start()

    loads[0].wait()
    launched(k_move, k_move_last, 4, 3)
    loads[2].wait()

    loads[4].wait()
    loads[5].wait()
    first = [jnp.int32(0), jnp.int32(0)]
    stop = [jnp.int32(0), jnp.int32(0)]
    at = jnp.int32(0)
    for j in range(tiles_ref.shape[0]):
        after = at + tiles_ref[j]
        end = after * TILE - pads_ref[j]
        for i in range(2):
            tile = 2 * mine + i
            inside = (at <= tile) & (tile < after)
            first[i] = jnp.where(inside, at, first[i])
            stop[i] = jnp.where(inside, end, stop[i])
        at = after

    def cols_of(i, c):
        return pl.ds(pl.multiple_of(i * cols + c * 2 * TILE, TILE), 2 * TILE)

    def two_heads(ref, i, c):
        at_row = pl.ds(i * TILE, TILE)
        return jnp.concatenate(
            [
                ref[at_row, pl.ds(pl.multiple_of((2 * c + n) * HEAD, HEAD), HEAD)]
                for n in range(2)
            ],
            axis=0,
        )

    def tiles_of(slot):
        return [i for i in range(2) if i <= slot <= AHEAD + i]

    def over_pairs(body, init=0):
        return lax.fori_loop(0, pairs, body, init, unroll=True)

    def scores(slot):
        def step(c, carry):
            key = kw[rows_of(slot)]
            for i in tiles_of(slot):
                s = jnp.dot(key, qt[:, cols_of(i, c)], preferred_element_type=F32)
                if slot == AHEAD + i:
                    row = lax.broadcasted_iota(jnp.int32, s.shape, 0)
                    col = lax.broadcasted_iota(jnp.int32, s.shape, 1)
                    s = jnp.where(row <= (col & (TILE - 1)), s, NEG)
                top = jnp.max(s, axis=0, keepdims=True) * c2
                w = jnp.exp2(s * c2 - top)
                e[rows_of(slot), cols_of(i, c)] = w
                m_ref[pl.ds(slot, 1), cols_of(i, c)] = top
                l_ref[pl.ds(slot, 1), cols_of(i, c)] = jnp.sum(w, axis=0, keepdims=True)
            return carry

        over_pairs(step)
        kt[:, rows_of(slot)] = jnp.transpose(kw[rows_of(slot)])

    def factors():
        for i in range(2):
            part = pl.ds(i * cols, cols)
            shape = (16, cols)
            row = lax.broadcasted_iota(jnp.int32, shape, 0)
            token = lax.broadcasted_iota(jnp.int32, shape, 1) & (TILE - 1)
            tile = 2 * mine + i
            valid = (row >= i) & (row <= AHEAD + i) & (row + (2 * mine - AHEAD) >= first[i])
            tops = jnp.where(valid, m_ref[:, part], NEG)
            w = jnp.exp2(tops - jnp.max(tops, axis=0, keepdims=True))
            total = jnp.sum(w * jnp.where(valid, l_ref[:, part], 0.0), axis=0, keepdims=True)
            live = token < stop[i] - tile * TILE
            f_ref[:, part] = jnp.where(live, w / total, 0.0)

    def value_part(slot):
        def step(c, acc):
            for i in tiles_of(slot):
                w = e[rows_of(slot), cols_of(i, c)] * f_ref[pl.ds(slot, 1), cols_of(i, c)]
                w = w.astype(BF16)
                p[rows_of(slot), cols_of(i, c)] = w
                acc = acc + jnp.dot(w, two_heads(g, i, c), preferred_element_type=F32)
                if slot in EARLY:
                    d = dp[rows_of(slot), cols_of(i, c)] * w.astype(F32)
                    d_ref[pl.ds(slot, 1), cols_of(i, c)] = jnp.sum(d, axis=0, keepdims=True)
            return acc

        return over_pairs(step, jnp.zeros((TILE, HEAD), F32))

    def dprobs_raw(slot):
        def step(c, carry):
            value = vw[rows_of(slot)]
            for i in tiles_of(slot):
                dp[rows_of(slot), cols_of(i, c)] = jnp.dot(
                    value, gt[:, cols_of(i, c)], preferred_element_type=F32
                )
            return carry

        over_pairs(step)

    def dprobs(slot):
        def step(c, carry):
            value = vw[rows_of(slot)]
            for i in tiles_of(slot):
                d = jnp.dot(value, gt[:, cols_of(i, c)], preferred_element_type=F32)
                dp[rows_of(slot), cols_of(i, c)] = d
                d = d * p[rows_of(slot), cols_of(i, c)].astype(F32)
                d_ref[pl.ds(slot, 1), cols_of(i, c)] = jnp.sum(d, axis=0, keepdims=True)
            return carry

        over_pairs(step)

    def deltas():
        for i in range(2):
            part = pl.ds(i * cols, cols)
            row = lax.broadcasted_iota(jnp.int32, (16, cols), 0)
            terms = jnp.where((row >= i) & (row <= AHEAD + i), d_ref[:, part], 0.0)
            f_ref[:, part] = jnp.broadcast_to(jnp.sum(terms, axis=0, keepdims=True), (16, cols))

    def key_part(slot):
        def step(c, acc):
            for i in tiles_of(slot):
                d = dp[rows_of(slot), cols_of(i, c)] - f_ref[pl.ds(0, 1), cols_of(i, c)]
                d = (p[rows_of(slot), cols_of(i, c)].astype(F32) * d).astype(BF16)
                p[rows_of(slot), cols_of(i, c)] = d
                acc = acc + jnp.dot(d, two_heads(q, i, c), preferred_element_type=F32)
            return acc

        return over_pairs(step, jnp.zeros((TILE, HEAD), F32)) * scale

    def query_part(i, dq):
        window = pl.ds(i * TILE, (SLOTS - 1) * TILE)

        def step(c, carry):
            t = jnp.dot(kt[:, window], p[window, cols_of(i, c)], preferred_element_type=F32) * scale
            for n in range(2):
                head = pl.ds(pl.multiple_of((2 * c + n) * HEAD, HEAD), HEAD)
                t_head = t[:, n * TILE : (n + 1) * TILE]
                dq[pl.ds(i * TILE, TILE), head] = jnp.transpose(t_head).astype(BF16)
            return carry

        over_pairs(step)

    def turned(ref, out):
        def step(c, carry):
            for i in range(2):
                for n in range(2):
                    head = pl.ds(pl.multiple_of((2 * c + n) * HEAD, HEAD), HEAD)
                    at_col = pl.ds(pl.multiple_of(i * cols + (2 * c + n) * TILE, TILE), TILE)
                    out[:, at_col] = jnp.transpose(ref[pl.ds(i * TILE, TILE), head])
            return carry

        over_pairs(step)

    def arrived(moves, *slots):
        for slot in slots:
            moves[slot].wait_recv()

    def relayed(moves):
        for slot, onward in ((4, (0, 2, 6)), (3, (1, 5))):
            moves[slot].wait_recv()
            for dst in onward:
                moves[dst].start()

    def sent(part, slot, moves, last, sbuf):
        sbuf[slot] = part.astype(BF16)
        moves[slot].start()
        if slot in (5, 6):
            last[slot].start()

    def added(part, slot, moves, last, sbuf, rbuf):
        for came in (1, 5) if slot == 3 else (2, 6, 0):
            moves[came].wait_recv()
            part = part + rbuf[came].astype(F32)
        sent(part, slot, moves, last, sbuf)

    def settled(parts, moves, rbuf, out):
        for slot in (7, 8):
            moves[slot - 4].wait_recv()
            part = parts[slot] + rbuf[slot - 4].astype(F32)
            out[rows_of(slot - AHEAD), :] = part.astype(BF16)

    loads[1].wait()
    turned(q, qt)
    scores(7)
    launched(v_move, v_move_last, 4, 3)
    scores(8)
    relayed(k_move)
    loads[3].wait()
    turned(g, gt)
    for slot in (3, 4):
        scores(slot)
    for slot in (7, 8):
        dprobs_raw(slot)
    relayed(v_move)
    for slot in (3, 4):
        dprobs_raw(slot)
    for slot in (2, 6, 0, 1, 5):
        arrived(k_move, slot)
        scores(slot)
    factors()

    v_part = {}
    for slot in (0, 2, 6, 1, 5):
        sent(value_part(slot), slot, v_home, v_home_last, sv)
    for slot in (3, 4, 7, 8):
        v_part[slot] = value_part(slot)
    for slot in (2, 6, 0, 1, 5):
        arrived(v_move, slot)
        dprobs(slot)
    deltas()

    k_part = {}
    for slot in (0, 2, 6, 1, 5):
        sent(key_part(slot), slot, k_home, k_home_last, sk)
    for slot in (3, 4, 7, 8):
        k_part[slot] = key_part(slot)
    query_part(0, dq_out)
    for slot in (4, 3):
        added(v_part[slot], slot, v_home, v_home_last, sv, rv)
    added(k_part[4], 4, k_home, k_home_last, sk, rk)
    added(k_part[3], 3, k_home, k_home_last, sk, rk)
    query_part(1, dq_out)
    settled(v_part, v_home, rv, dv_out)
    settled(k_part, k_home, rk, dk_out)

    for moves in (k_move, v_move, v_home, k_home):
        for move in moves:
            move.wait_send()
    for moves in (k_move_last, v_move_last, v_home_last, k_home_last):
        for move in moves.values():
            move.wait_send()


def store(dq, dk, dv, dq_out, dk_out, dv_out, sem):
    moves = [
        pltpu.make_async_copy(src, dst, sem.at[n])
        for n, (src, dst) in enumerate(((dq, dq_out), (dk, dk_out), (dv, dv_out)))
    ]
    for move in moves:
        move.start()
    for move in moves:
        move.wait()


def shards(queries, keys, values, output_gradient, doc_tiles, doc_pads):
    rows, wide = queries.shape
    window = SLOTS * TILE
    both = 2 * (wide // HEAD) * TILE
    anywhere = pl.BlockSpec(memory_space=pl.ANY)
    vmem = pl.BlockSpec(memory_space=pltpu.VMEM)
    dma = pltpu.SemaphoreType.DMA
    operands = (doc_tiles, doc_pads, queries, keys, values, output_gradient)
    shapes = tuple(jax.ShapeDtypeStruct(x.shape, BF16) for x in (queries, keys, values))
    grads = pl.pallas_call(
        kernel,
        out_shape=shapes,
        in_specs=[anywhere] * 6,
        out_specs=(vmem, vmem, vmem),
        scratch_shapes=[
            pltpu.SMEM(doc_tiles.shape, jnp.int32),
            pltpu.SMEM(doc_pads.shape, jnp.int32),
            pltpu.VMEM((rows, wide), BF16),
            pltpu.VMEM((rows, wide), BF16),
            pltpu.VMEM((HEAD, both), BF16),
            pltpu.VMEM((HEAD, both), BF16),
            pltpu.VMEM((window, HEAD), BF16),
            pltpu.VMEM((window, HEAD), BF16),
            pltpu.VMEM((HEAD, window), BF16),
            pltpu.VMEM((window, both), F32),
            pltpu.VMEM((window, both), F32),
            pltpu.VMEM((window, both), BF16),
            pltpu.VMEM((16, both), F32),
            pltpu.VMEM((16, both), F32),
            pltpu.VMEM((16, both), F32),
            pltpu.VMEM((16, both), F32),
        ]
        + [pltpu.VMEM((AHEAD, TILE, HEAD), BF16)] * 4
        + [dma((6,))]
        + [dma((AHEAD,))] * 8,
        compiler_params=pltpu.CompilerParams(
            collective_id=0, has_side_effects=True, vmem_limit_bytes=48 * 1024 * 1024
        ),
        cost_estimate=pl.CostEstimate(flops=2_700_000_000, bytes_accessed=2_400_000, transcendentals=2_100_000),
        name="attention_backward",
    )(*[pltpu.with_memory_space_constraint(x, pltpu.HBM) for x in operands])
    return pl.pallas_call(
        store,
        out_shape=shapes,
        in_specs=[vmem] * 3,
        out_specs=(anywhere,) * 3,
        scratch_shapes=[dma((3,))],
        name="store_gradients",
    )(*[pltpu.with_memory_space_constraint(x, pltpu.VMEM) for x in grads])


def solution(mesh):
    split = P(("ctx", "grp"), "tp")
    return jax.shard_map(
        shards,
        mesh=mesh,
        in_specs=(split, split, split, split, P(), P()),
        out_specs=(split, split, split),
        check_vma=False,
    )
```
